32 devices in a mesh: row: 8 (over z, core), col: 4 (over y, x).
Axes of the slice: x: 2, y: 2, z: 4, core: 2. Of those that a mesh axis runs over, the one named last changes fastest.
Arguments:
- rhs_top: bfloat16 [2, 1024, 4096], P(None, 'row', 'col'), may hold values from -6 to 6
- diag_inverse: bfloat16 [2, 1024, 1024], P(None, 'row'), as said below
- panel_coupling: bfloat16 [1024, 1024], P('row'), may hold values from -0.1875 to 0.1875
- trailing_factor: bfloat16 [8192, 2048], P('row', 'col'), may hold values from -0.125 to 0.125
- rhs_trailing: bfloat16 [8192, 4096], P('row', 'col'), may hold values from -6 to 6
Outputs:
- solved: bfloat16 [2, 1024, 4096], P(None, 'row', 'col')
- updated: bfloat16 [8192, 4096], P('row', 'col')
The draws below stay inside these ranges and needn't reach their ends.
Inputs may be any that keep to these rules, and one draw needn't show every extreme that they name: Each diag_inverse[k] is lower triangular.
All inputs are finite; a program needn't handle non-finite values.
Results may differ from the reference program's by a relative error of at most 0.0055.
Values may be sent and summed in bfloat16 or wider, within the bound.
No kernel may reach another device: no remote copies, remote signals or barrier semaphores. Data moves between devices by JAX's collectives and lax.ppermute only.
A program may use at most 64 MiB of HBM per device.

```python
import jax
import jax.numpy as jnp
from jax import lax

PB = 1024
ROWS_DEV = 1024
ROWS = 8192
NRHS = 4096


def draw_diag_inverse(key, part):
    key_off, key_diag = jax.random.split(jax.random.fold_in(key, 17))
    rows = lax.broadcasted_iota(jnp.int32, (2, PB, PB), 1)
    cols = lax.broadcasted_iota(jnp.int32, (2, PB, PB), 2)
    off = jax.random.normal(key_off, (2, PB, PB), jnp.float32) * (0.6 * PB ** (-0.5))
    diag = jax.random.uniform(key_diag, (2, PB, PB), jnp.float32, 0.6, 1.4)
    whole = jnp.where(rows > cols, off, jnp.where(rows == cols, diag, jnp.zeros_like(off)))
    return whole.astype(jnp.bfloat16)


def block_scale(key, shape, cuts, smallest, top_value):
    factor_of, own = 1.0, jax.random.fold_in(key, 6)
    for axis_at, blocks in cuts:
        heights = jnp.exp(jax.random.uniform(jax.random.fold_in(own, axis_at), (blocks,), jnp.float32, smallest / len(cuts), top_value / len(cuts)))
        factor_of = factor_of * jnp.repeat(heights, shape[axis_at] // blocks).reshape([-1 if axis == axis_at else 1 for axis in range(len(shape))])
    return factor_of


def bell_draw(key, extent, width, reach, cuts=(), kind=jnp.bfloat16):
    values = jax.random.normal(key, extent, jnp.float32) * width
    if len(cuts) > 0:
        values = block_scale(key, extent, cuts, -0.22, 0.18) * values
    return jnp.clip(values, min=-reach, max=reach).astype(kind)


def setup_inputs(seed: int = 0) -> dict:
    splits = jax.random.split(jax.random.key(seed), 6)
    rhs_top = bell_draw(splits[0], (2, PB, NRHS), 1.0, 6.0, ((1, 8), (2, 4)))
    diag_inverse = draw_diag_inverse(jax.random.fold_in(splits[5], 71), 0)
    panel_coupling = bell_draw(splits[2], (PB, PB), PB ** -0.5, 0.1875, ((0, 8),))
    trailing_factor = bell_draw(splits[3], (ROWS, 2 * PB), (2 * PB) ** -0.5, 0.125, ((0, 8), (1, 4)))
    rhs_trailing = bell_draw(splits[4], (ROWS, NRHS), 1.0, 6.0, ((0, 8), (1, 4)))
    return {"rhs_top": rhs_top, "diag_inverse": diag_inverse, "panel_coupling": panel_coupling, "trailing_factor": trailing_factor, "rhs_trailing": rhs_trailing}


def reference(rhs_top, diag_inverse, panel_coupling, trailing_factor, rhs_trailing):
    first = jnp.dot(diag_inverse[0], rhs_top[0], preferred_element_type=jnp.float32).astype(jnp.bfloat16)
    carried = (rhs_top[1].astype(jnp.float32) - jnp.dot(panel_coupling, first, preferred_element_type=jnp.float32)).astype(jnp.bfloat16)
    second = jnp.dot(diag_inverse[1], carried, preferred_element_type=jnp.float32).astype(jnp.bfloat16)
    solution = jnp.concatenate([first, second], axis=0)
    blocks = ROWS // ROWS_DEV
    factor_blocks = trailing_factor.reshape(blocks, ROWS_DEV, 2 * PB)
    rhs_blocks = rhs_trailing.reshape(blocks, ROWS_DEV, NRHS)

    def update(pair):
        factor_rows, rhs_rows = pair
        product = jnp.dot(factor_rows, solution, preferred_element_type=jnp.float32)
        return (rhs_rows.astype(jnp.float32) - product).astype(jnp.bfloat16)

    updated = lax.map(update, (factor_blocks, rhs_blocks)).reshape(ROWS, NRHS)
    return jnp.stack([first, second]), updated
```

```python
import functools

import jax
import jax.numpy as jnp
from jax import lax
from jax.experimental import pallas as pl
from jax.experimental.pallas import tpu as pltpu
from jax.sharding import PartitionSpec as P

VMEM_BYTES = 40 * 1024 * 1024


def bits_of(size):
    return [1 << b for b in reversed(range(size.bit_length() - 1))]


def send(x, sizes, to):
    rows, cols = sizes
    pairs = []
    for r in range(rows):
        for c in range(cols):
            there_r, there_c = to(r, c)
            pairs.append((r * cols + c, there_r * cols + there_c))
    return lax.ppermute(x, ("row", "col"), pairs)


def swap_cores(x, sizes):
    return send(x, sizes, lambda r, c: (r ^ 1, c))


def gather_line(x, sizes):
    chips = sizes[0] // 2
    held = {0: x}
    for bit in bits_of(chips):
        for s in list(held):
            held[s | bit] = send(held[s], sizes, lambda r, c: (r ^ (2 * bit), c))
    return [held[s] for s in range(chips)]


def plane_bits(cols, core):
    bits = bits_of(cols)
    return bits[::-1] if core == 0 else bits


def gather_plane(x, sizes):
    cols = sizes[1]
    held = [x]
    for i in range(len(bits_of(cols))):
        held += [
            send(h, sizes, lambda r, c: (r, c ^ plane_bits(cols, r % 2)[i])) for h in held
        ]
    return held


def plane_owner(c, m, cols, core):
    offsets = []
    for which in (0, 1):
        bits = plane_bits(cols, which)
        offsets.append(sum(bit for i, bit in enumerate(bits) if m >> i & 1))
    return c ^ jnp.where(core == 0, offsets[0], offsets[1])


def load_all(copies):
    for copy in copies:
        copy.start()
    for copy in copies:
        copy.wait()


def lower_product(inverse, right, out_ref, step):
    pb = inverse.shape[0]
    for top in range(0, pb, step):
        depth = top + step
        out_ref[top:depth, :] = jnp.dot(
            inverse[top:depth, :depth], right[:depth, :], preferred_element_type=jnp.float32
        ).astype(out_ref.dtype)


def inverse_copies(place, mine, theirs, inverse, sems, rows_dev, cols):
    z, k, c = place
    copies = []
    for packs, core in ((mine, k), (theirs, 1 - k)):
        for m, pack in enumerate(packs):
            owner = plane_owner(c, m, cols, core)
            chips, height, _ = pack.shape
            for s in range(chips):
                top = (z ^ s) * 2 * rows_dev + core * rows_dev + owner * height
                copies.append(
                    pltpu.make_async_copy(
                        pack.at[s],
                        inverse.at[pl.ds(pl.multiple_of(top, height), height), :],
                        sems.at[len(copies)],
                    )
                )
    return copies


def right_copies(place, blocks, right, sems, rows_dev, base):
    z, k, _ = place
    copies = []
    for s, block in enumerate(blocks):
        for part, core in ((0, k), (1, 1 - k)):
            top = (z ^ s) * 2 * rows_dev + core * rows_dev
            copies.append(
                pltpu.make_async_copy(
                    block.at[part * rows_dev : (part + 1) * rows_dev, :],
                    right.at[pl.ds(pl.multiple_of(top, rows_dev), rows_dev), :],
                    sems.at[base + len(copies)],
                )
            )
    return copies


def solve_kernel(chips, cols, rows_dev, carry, *refs):
    place_ref, refs = refs[0], refs[1:]
    place = tuple(place_ref[i] for i in range(3))
    mine, theirs, refs = refs[:cols], refs[cols : 2 * cols], refs[2 * cols :]
    blocks, refs = refs[:chips], refs[chips:]
    if carry:
        coupling, below, out_ref, carried_ref, inverse, right, sems = refs
    else:
        out_ref, inverse, right, sems = refs
    copies = inverse_copies(place, mine, theirs, inverse, sems, rows_dev, cols)
    copies += right_copies(place, blocks, right, sems, rows_dev, len(copies))
    load_all(copies)
    lower_product(inverse, right, out_ref, min(256, 2 * rows_dev))
    if carry:
        carried_ref[...] = (
            below[...].astype(jnp.float32)
            - jnp.dot(coupling[...], out_ref[...], preferred_element_type=jnp.float32)
        ).astype(carried_ref.dtype)


def solve(place, mine, theirs, blocks, sizes, rows_dev, pb, extra=()):
    chips, cols = sizes[0] // 2, sizes[1]
    width = blocks[0].shape[1]
    n_copies = 2 * cols * chips + 2 * chips
    any_spec = pl.BlockSpec(memory_space=pl.ANY)
    vmem = pl.BlockSpec(memory_space=pltpu.VMEM)
    out_shape = [jax.ShapeDtypeStruct((pb, width), jnp.bfloat16)]
    if extra:
        out_shape.append(jax.ShapeDtypeStruct((2 * rows_dev, width), jnp.bfloat16))
    return pl.pallas_call(
        functools.partial(solve_kernel, chips, cols, rows_dev, bool(extra)),
        out_shape=out_shape,
        in_specs=[pl.BlockSpec(memory_space=pltpu.SMEM)]
        + [any_spec] * (2 * cols + chips)
        + [vmem] * len(extra),
        out_specs=[vmem] * len(out_shape),
        scratch_shapes=[
            pltpu.VMEM((pb, pb), jnp.bfloat16),
            pltpu.VMEM((pb, width), jnp.bfloat16),
            pltpu.SemaphoreType.DMA((n_copies,)),
        ],
        compiler_params=pltpu.CompilerParams(vmem_limit_bytes=VMEM_BYTES),
    )(place, *mine, *theirs, *blocks, *extra)


def trailing_kernel(cols, rows_dev, place_ref, *refs):
    z, k, c = (place_ref[i] for i in range(3))
    factors, refs = refs[:cols], refs[cols:]
    x_mine, x_theirs, refs = refs[:2], refs[2:4], refs[4:]
    rhs, updated, solved, factor, x, sems = refs
    pb, width = x_mine[0].shape
    chunk = factors[0].shape[1]
    copies = []
    for m, block in enumerate(factors):
        left = pl.multiple_of(plane_owner(c, m, cols, k) * chunk, chunk)
        copies.append(
            pltpu.make_async_copy(block, factor.at[:, pl.ds(left, chunk)], sems.at[len(copies)])
        )
    for parts, core in ((x_mine, k), (x_theirs, 1 - k)):
        left = pl.multiple_of(core * width, width)
        for panel, part in enumerate(parts):
            copies.append(
                pltpu.make_async_copy(
                    part,
                    x.at[panel * pb : (panel + 1) * pb, pl.ds(left, width)],
                    sems.at[len(copies)],
                )
            )
    load_all(copies)
    top = pl.multiple_of((2 * z + k) * rows_dev, rows_dev)
    for panel in range(2):
        solved[panel] = x[pl.ds(panel * pb + top, rows_dev), :]
    step = min(256, rhs.shape[0])
    for at in range(0, rhs.shape[0], step):
        updated[at : at + step, :] = (
            rhs[at : at + step, :].astype(jnp.float32)
            - jnp.dot(factor[at : at + step, :], x[...], preferred_element_type=jnp.float32)
        ).astype(updated.dtype)


def trailing(place, factors, x_mine, x_theirs, rhs, rows_dev):
    cols = len(factors)
    pb, width = x_mine[0].shape
    any_spec = pl.BlockSpec(memory_space=pl.ANY)
    vmem = pl.BlockSpec(memory_space=pltpu.VMEM)
    return pl.pallas_call(
        functools.partial(trailing_kernel, cols, rows_dev),
        out_shape=[
            jax.ShapeDtypeStruct(rhs.shape, jnp.bfloat16),
            jax.ShapeDtypeStruct((2, rows_dev, 2 * width), jnp.bfloat16),
        ],
        in_specs=[pl.BlockSpec(memory_space=pltpu.SMEM)] + [any_spec] * (cols + 4) + [vmem],
        out_specs=[vmem, vmem],
        scratch_shapes=[
            pltpu.VMEM((rhs.shape[0], cols * factors[0].shape[1]), jnp.bfloat16),
            pltpu.VMEM((2 * pb, 2 * width), jnp.bfloat16),
            pltpu.SemaphoreType.DMA((cols + 4,)),
        ],
        compiler_params=pltpu.CompilerParams(vmem_limit_bytes=VMEM_BYTES),
    )(place, *factors, *x_mine, *x_theirs, rhs)


def by_permutes(sizes, rhs_top, diag_inverse, panel_coupling, trailing_factor, rhs_trailing):
    rows, cols = sizes
    rows_dev, pb = diag_inverse.shape[1:]
    half = rhs_top.shape[2] // 2
    r, c = lax.axis_index("row"), lax.axis_index("col")
    z, k = r // 2, r % 2
    place = jnp.stack([z, k, c]).astype(jnp.int32)

    mine = lax.dynamic_slice_in_dim(rhs_top, k * half, half, 2)
    theirs = swap_cores(lax.dynamic_slice_in_dim(rhs_top, (1 - k) * half, half, 2), sizes)
    chip_rhs = jnp.concatenate([mine, theirs], axis=1)
    chip_coupling = jnp.concatenate([panel_coupling, swap_cores(panel_coupling, sizes)], axis=0)

    height = rows_dev // cols
    share = lax.dynamic_slice_in_dim(diag_inverse, c * height, height, 1)
    packs, their_packs = [], []
    for panel in range(2):
        pack = jnp.stack(gather_line(share[panel], sizes))
        packs.append(gather_plane(pack, sizes))
        their_packs.append([swap_cores(p, sizes) for p in packs[-1]])
    factors = gather_plane(trailing_factor, sizes)

    blocks = gather_line(chip_rhs[0], sizes)
    first, carried = solve(
        place, packs[0], their_packs[0], blocks, sizes, rows_dev, pb, (chip_coupling, chip_rhs[1])
    )
    first_theirs = swap_cores(first, sizes)
    blocks = gather_line(carried, sizes)
    (second,) = solve(place, packs[1], their_packs[1], blocks, sizes, rows_dev, pb)
    second_theirs = swap_cores(second, sizes)
    updated, solved = trailing(
        place, factors, (first, second), (first_theirs, second_theirs), rhs_trailing, rows_dev
    )
    return solved, updated


def by_gathers(rhs_top, diag_inverse, panel_coupling, trailing_factor, rhs_trailing):
    def product(left, right):
        return jnp.dot(left, right, preferred_element_type=jnp.float32)

    def whole(x):
        return lax.all_gather(x, "row", axis=0, tiled=True)

    first = product(diag_inverse[0], whole(rhs_top[0])).astype(jnp.bfloat16)
    first_all = whole(first)
    carried = rhs_top[1].astype(jnp.float32) - product(panel_coupling, first_all)
    second = product(diag_inverse[1], whole(carried.astype(jnp.bfloat16))).astype(jnp.bfloat16)
    x = jnp.concatenate([first_all, whole(second)], axis=0)
    factor = lax.all_gather(trailing_factor, "col", axis=1, tiled=True)
    updated = (rhs_trailing.astype(jnp.float32) - product(factor, x)).astype(jnp.bfloat16)
    return jnp.stack([first, second]), updated


def fits(sizes, rhs_top, diag_inverse):
    rows, cols = sizes
    powers = rows >= 2 and rows & (rows - 1) == 0 and cols & (cols - 1) == 0
    return powers and diag_inverse.shape[1] % (16 * cols) == 0 and rhs_top.shape[2] % 256 == 0


def solution(mesh):
    sizes = (mesh.shape["row"], mesh.shape["col"])

    def shards(rhs_top, diag_inverse, *others):
        if fits(sizes, rhs_top, diag_inverse):
            return by_permutes(sizes, rhs_top, diag_inverse, *others)
        return by_gathers(rhs_top, diag_inverse, *others)

    in_specs = (
        P(None, "row", "col"),
        P(None, "row", None),
        P("row", None),
        P("row", "col"),
        P("row", "col"),
    )
    out_specs = (P(None, "row", "col"), P("row", "col"))
    return jax.shard_map(shards, mesh=mesh, in_specs=in_specs, out_specs=out_specs, check_vma=False)
```

```python
import functools

import jax
import jax.numpy as jnp
from jax import lax
from jax.experimental import pallas as pl
from jax.experimental.pallas import tpu as pltpu
from jax.sharding import PartitionSpec as P

VMEM_BYTES = 40 * 1024 * 1024

CHUNKS = 1


def bits_of(size):
    return [1 << b for b in reversed(range(size.bit_length() - 1))]


def send(x, sizes, to):
    rows, cols = sizes
    pairs = []
    for r in range(rows):
        for c in range(cols):
            there_r, there_c = to(r, c)
            pairs.append((r * cols + c, there_r * cols + there_c))
    return lax.ppermute(x, ("row", "col"), pairs)


def after(x, *done):
    return lax.optimization_barrier((x, done))[0]


def plane_bits(cols, core):
    bits = bits_of(cols)
    return bits[::-1] if core == 0 else bits


def plane_owner(c, m, cols, core):
    offsets = []
    for which in (0, 1):
        bits = plane_bits(cols, which)
        offsets.append(sum(bit for i, bit in enumerate(bits) if m >> i & 1))
    return c ^ jnp.where(core == 0, offsets[0], offsets[1])


def product(left, right):
    return jnp.dot(left, right, preferred_element_type=jnp.float32)


def cost_of(us):
    return pl.CostEstimate(flops=us * 10**9, transcendentals=0, bytes_accessed=0) if us else None


def call(kernel, out_shape, place, *operands, scratch_shapes=(), cost=None, outputs=pltpu.VMEM):
    vmem = pl.BlockSpec(memory_space=pltpu.VMEM)
    return pl.pallas_call(
        kernel,
        out_shape=out_shape,
        in_specs=[pl.BlockSpec(memory_space=pltpu.SMEM)] + [vmem] * len(operands),
        out_specs=jax.tree.map(lambda _: pl.BlockSpec(memory_space=outputs), out_shape),
        scratch_shapes=scratch_shapes,
        cost_estimate=cost,
        compiler_params=pltpu.CompilerParams(vmem_limit_bytes=VMEM_BYTES),
    )(place, *operands)


def tri_at(z, wide):
    return wide * (z * (z + 1) // 2)


def pack_kernel(place_ref, *refs):
    pieces, out_ref = refs[:-1], refs[-1]
    chips, wide = len(pieces), pieces[0].shape[1] // len(pieces)
    height = out_ref.shape[0]
    for s in range(chips):
        for owner in range(chips):

            @pl.when(place_ref[0] ^ s == owner)
            def _(s=s, owner=owner):
                depth = wide * (owner + 1)
                for panel in range(2):
                    left = panel * tri_at(chips, wide) + tri_at(owner, wide)
                    rows = slice(panel * height, (panel + 1) * height)
                    out_ref[:, left : left + depth] = pieces[s][rows, :depth]


def pack_rows(place, pieces, cost):
    height, pb = pieces[0].shape[0] // 2, pieces[0].shape[1]
    width = 2 * tri_at(len(pieces), pb // len(pieces))
    out_shape = jax.ShapeDtypeStruct((height, width), jnp.bfloat16)
    return call(pack_kernel, out_shape, place, *pieces, cost=cost_of(cost))


def unpack_kernel(chips, rows_dev, place_ref, *refs):
    packs, out_ref = refs[:-1], refs[-1]
    cols = len(packs) // 2
    k, c = place_ref[1], place_ref[2]
    height, wide = packs[0].shape[0], out_ref.shape[2] // chips
    for at, pack in enumerate(packs):
        core = k if at < cols else 1 - k
        row = core * rows_dev + plane_owner(c, at % cols, cols, core) * height
        for z in range(chips):
            rows = pl.ds(pl.multiple_of(z * 2 * rows_dev + row, height), height)
            for panel in range(2):
                left, depth = panel * tri_at(chips, wide) + tri_at(z, wide), wide * (z + 1)
                out_ref[panel, rows, :depth] = pack[:, left : left + depth]


def unpack_rows(place, packs, chips, rows_dev, pb):
    out_shape = jax.ShapeDtypeStruct((2, pb, pb), jnp.bfloat16)
    return call(functools.partial(unpack_kernel, chips, rows_dev), out_shape, place, *packs)


def lower_product(place_ref, inverse, blocks, out_ref, right):
    z, k = place_ref[0], place_ref[1]
    rows_dev = blocks[0].shape[0] // 2
    for s, block in enumerate(blocks):
        for part, core in ((0, k), (1, 1 - k)):
            row = pl.multiple_of((z ^ s) * 2 * rows_dev + core * rows_dev, rows_dev)
            right[pl.ds(row, rows_dev), :] = block[part * rows_dev : (part + 1) * rows_dev, :]
    step = 2 * rows_dev
    for top in range(0, right.shape[0], step):
        out_ref[top : top + step, :] = product(
            inverse[top : top + step, : top + step], right[: top + step, :]
        ).astype(out_ref.dtype)


def first_kernel(place_ref, inverse, mine, theirs, below, *refs):
    blocks, (first, *carried, right) = refs[: -2 - CHUNKS], refs[-2 - CHUNKS :]
    lower_product(place_ref, inverse.at[0], blocks, first, right)
    width = carried[0].shape[1]
    rows_dev = mine.shape[0]
    for part, coupling in enumerate((mine, theirs)):
        rows = slice(part * rows_dev, (part + 1) * rows_dev)
        new = below[rows, :].astype(jnp.float32) - product(coupling[...], first[...])
        for chunk, out in enumerate(carried):
            out[rows, :] = new[:, chunk * width : (chunk + 1) * width].astype(out.dtype)


def second_kernel(place_ref, inverse, *refs):
    blocks, (second, right) = refs[:-2], refs[-2:]
    lower_product(place_ref, inverse.at[1], blocks, second, right)


def trailing_rows(panel, place_ref, total, factors, mine, theirs, out, done=None):
    k, c = place_ref[1], place_ref[2]
    cols = len(factors)
    depth, width = factors[0].shape[1], out.shape[1] // 2
    step, wide = min(256, out.shape[0]), mine[0].shape[1]
    for which in (0, 1):
        for upper in (0, 1):

            @pl.when(jnp.logical_and(k == which, c // (cols // 2) == upper))
            def _(which=which, upper=upper):
                at = plane_bits(cols, which).index(cols // 2)
                held = [m for m in range(cols) if m >> at & 1 == upper ^ panel]
                tops = [plane_owner(c, m, cols, which) % (cols // 2) * depth for m in held]
                tops = [pl.multiple_of(top, depth) for top in tops]
                for top in range(0, out.shape[0], step):
                    rows = slice(top, top + step)
                    left = jnp.concatenate([factors[m][rows, :] for m in held], axis=1)
                    for x, core in ((mine, which), (theirs, 1 - which)):
                        for chunk, part in enumerate(x):
                            right = [part[pl.ds(row, depth), :] for row in tops]
                            left_at = core * width + chunk * wide
                            columns = slice(left_at, left_at + wide)
                            out[rows, columns] = (
                                total[rows, columns].astype(jnp.float32)
                                - product(left, jnp.concatenate(right, axis=0))
                            ).astype(out.dtype)
                    if done:
                        done(rows)


def total_kernel(place_ref, rhs, *refs):
    factors, (mine, theirs, total) = refs[:-3], refs[-3:]
    trailing_rows(0, place_ref, rhs, factors, [mine], [theirs], total)


def last_kernel(place_ref, total, first, first_theirs, *refs):
    updated, solved, new_rows, new_solved, row_sems, solved_sem = refs[-6:]
    factors, x = refs[: -6 - 2 * CHUNKS], refs[-6 - 2 * CHUNKS : -6]
    second, second_theirs = x[:CHUNKS], x[CHUNKS:]
    z, k = place_ref[0], place_ref[1]
    rows_dev, width = solved.shape[1], first.shape[1]
    own = pl.ds(pl.multiple_of((2 * z + k) * rows_dev, rows_dev), rows_dev)
    panels = (([first], [first_theirs]), (second, second_theirs))
    for panel, halves in enumerate(panels):
        for half, core in zip(halves, (k, 1 - k)):
            wide = half[0].shape[1]
            for chunk, part in enumerate(half):
                left = pl.multiple_of(core * width + chunk * wide, wide)
                new_solved[panel, :, pl.ds(left, wide)] = part[own, :]
    store_solved = pltpu.make_async_copy(new_solved, solved, solved_sem)
    store_solved.start()
    step = updated.shape[0] // row_sems.shape[0]

    def store(rows):
        return pltpu.make_async_copy(
            new_rows.at[rows], updated.at[rows], row_sems.at[rows.start // step]
        )

    def done(rows):
        store(rows).start()

    trailing_rows(1, place_ref, total, factors, second, second_theirs, new_rows, done)
    for top in range(0, updated.shape[0], step):
        store(slice(top, top + step)).wait()
    store_solved.wait()


def by_permutes(sizes, rhs_top, diag_inverse, panel_coupling, trailing_factor, rhs_trailing):
    rows, cols = sizes
    chips = rows // 2
    rows_dev, pb = diag_inverse.shape[1:]
    half = rhs_top.shape[2] // 2
    wide = half // CHUNKS
    height = rows_dev // cols
    r, c = lax.axis_index("row"), lax.axis_index("col")
    z, k = r // 2, r % 2
    place = jnp.stack([z, k, c]).astype(jnp.int32)
    far, near = bits_of(chips)

    def along(x, s):
        return send(x, sizes, lambda r, c: (r ^ (2 * s), c))

    def across(x, i):
        return send(x, sizes, lambda r, c: (r, c ^ plane_bits(cols, r % 2)[i]))

    def swap(x):
        return send(x, sizes, lambda r, c: (r ^ 1, c))

    def block(*shape, dtype=jnp.bfloat16):
        return jax.ShapeDtypeStruct(shape, dtype)

    def share_of(matrices):
        mine = lax.dynamic_slice_in_dim(matrices, c * height, height, 1)
        return mine.reshape(2 * height, pb)

    def columns(core):
        return lax.dynamic_slice_in_dim(rhs_top, core * half, half, 2)

    def first_and_carried(*args):
        return call(
            first_kernel,
            [block(pb, half)] + [block(2 * rows_dev, wide)] * CHUNKS,
            place,
            *args,
            scratch_shapes=[pltpu.VMEM((pb, half), jnp.bfloat16)],
            cost=cost_of(0),
        )

    def second_of(*args):
        scratch = [pltpu.VMEM((pb, wide), jnp.bfloat16)]
        return call(second_kernel, block(pb, wide), place, *args, scratch_shapes=scratch)

    def total_of(*args):
        out_shape = block(*rhs_trailing.shape, dtype=jnp.float32)
        return call(total_kernel, out_shape, place, rhs_trailing, *args, cost=cost_of(4))

    def outputs_of(*args):
        out_shape = [block(*rhs_trailing.shape), block(2, rows_dev, 2 * half)]
        n_stores = max(rhs_trailing.shape[0] // 256, 1)
        scratch = [pltpu.VMEM(out.shape, out.dtype) for out in out_shape]
        scratch += [pltpu.SemaphoreType.DMA((n_stores,)), pltpu.SemaphoreType.DMA]
        return call(last_kernel, out_shape, place, *args, scratch_shapes=scratch, outputs=pl.ANY)

    share = share_of(diag_inverse)
    share_far = along(share, far)
    share_near = along(share, near)
    share_last = along(after(share_far, share_near), near)
    pack = pack_rows(place, [share, share_near, share_far, share_last], 2)
    pack_a = across(pack, 0)
    pack_b = across(pack, 1)
    pack_theirs = swap(pack)
    pack_a_theirs = swap(pack_a)
    pack_b_theirs = swap(pack_b)
    swapped = swap(columns(1 - k))
    chip_rhs = jnp.concatenate([columns(k), swapped], axis=1)
    top_far = along(after(chip_rhs, share_far)[0], far)
    top_near = along(after(chip_rhs, share_last)[0], near)
    top_last = along(top_far, near)
    coupling_theirs = swap(after(panel_coupling, top_far))
    pack_ab = across(after(pack_a, (coupling_theirs, pack_b, top_near)), 1)
    pack_ab_theirs = swap(pack_ab)
    inverse = unpack_rows(
        place,
        [
            pack,
            pack_a,
            pack_b,
            pack_ab,
            pack_theirs,
            pack_a_theirs,
            pack_b_theirs,
            after(pack_ab_theirs,
            top_last),
        ],
        chips,
        rows_dev,
        pb,
    )
    first_carried = first_and_carried(
        inverse,
        panel_coupling,
        coupling_theirs,
        chip_rhs[1],
        chip_rhs[0],
        top_near,
        top_far,
        top_last,
    )
    first = first_carried[0]
    first_theirs = swap(after(first, top_last))
    carried_0 = first_carried[1]
    carried_far_0 = along(carried_0, far)
    carried_near_0 = along(carried_0, near)
    factor_a = across(after(trailing_factor, share), 0)
    factor_b = across(after(trailing_factor, (coupling_theirs, factor_a)), 1)
    carried_last_0 = along(after(carried_far_0, (carried_near_0, factor_b, first_theirs)), near)
    second_0 = second_of(inverse, carried_0, carried_near_0, carried_far_0, carried_last_0)
    second_0_theirs = swap(second_0)
    factor_ab = across(after(factor_a, (factor_b, pack_ab)), 1)
    total = total_of(trailing_factor, factor_a, factor_b, factor_ab, first, first_theirs)
    outputs = outputs_of(
        total,
        first,
        first_theirs,
        trailing_factor,
        factor_a,
        factor_b,
        factor_ab,
        second_0,
        second_0_theirs,
    )
    updated, solved = outputs
    return solved, updated


def by_gathers(rhs_top, diag_inverse, panel_coupling, trailing_factor, rhs_trailing):
    def whole(x):
        return lax.all_gather(x, "row", axis=0, tiled=True)

    first = product(diag_inverse[0], whole(rhs_top[0])).astype(jnp.bfloat16)
    first_all = whole(first)
    carried = rhs_top[1].astype(jnp.float32) - product(panel_coupling, first_all)
    second = product(diag_inverse[1], whole(carried.astype(jnp.bfloat16))).astype(jnp.bfloat16)
    x = jnp.concatenate([first_all, whole(second)], axis=0)
    factor = lax.all_gather(trailing_factor, "col", axis=1, tiled=True)
    updated = (rhs_trailing.astype(jnp.float32) - product(factor, x)).astype(jnp.bfloat16)
    return jnp.stack([first, second]), updated


def fits(sizes, rhs_top, diag_inverse):
    rows, cols = sizes
    whole_rows = diag_inverse.shape[1] % (16 * cols) == 0
    whole_columns = diag_inverse.shape[2] % (64 * rows) == 0 and rhs_top.shape[2] % 256 == 0
    return rows == 8 and cols == 4 and whole_rows and whole_columns


def solution(mesh):
    sizes = (mesh.shape["row"], mesh.shape["col"])

    def shards(rhs_top, diag_inverse, *others):
        if fits(sizes, rhs_top, diag_inverse):
            return by_permutes(sizes, rhs_top, diag_inverse, *others)
        return by_gathers(rhs_top, diag_inverse, *others)

    in_specs = (
        P(None, "row", "col"),
        P(None, "row", None),
        P("row", None),
        P("row", "col"),
        P("row", "col"),
    )
    out_specs = (P(None, "row", "col"), P("row", "col"))
    return jax.shard_map(shards, mesh=mesh, in_specs=in_specs, out_specs=out_specs, check_vma=False)
```

```python
import functools

import jax
import jax.numpy as jnp
from jax import lax
from jax.experimental import pallas as pl
from jax.experimental.pallas import tpu as pltpu
from jax.sharding import PartitionSpec as P

VMEM_BYTES = 40 * 1024 * 1024

CHUNKS = 1


def bits_of(size):
    return [1 << b for b in reversed(range(size.bit_length() - 1))]


def send(x, sizes, to):
    rows, cols = sizes
    pairs = []
    for r in range(rows):
        for c in range(cols):
            there_r, there_c = to(r, c)
            pairs.append((r * cols + c, there_r * cols + there_c))
    return lax.ppermute(x, ("row", "col"), pairs)


def after(x, *done):
    return lax.optimization_barrier((x, done))[0]


def plane_bits(cols, core):
    bits = bits_of(cols)
    return bits[::-1] if core == 0 else bits


def plane_owner(c, m, cols, core):
    offsets = []
    for which in (0, 1):
        bits = plane_bits(cols, which)
        offsets.append(sum(bit for i, bit in enumerate(bits) if m >> i & 1))
    return c ^ jnp.where(core == 0, offsets[0], offsets[1])


def product(left, right):
    return jnp.dot(left, right, preferred_element_type=jnp.float32)


def cost_of(us):
    return pl.CostEstimate(flops=us * 10**9, transcendentals=0, bytes_accessed=0) if us else None


def call(kernel, out_shape, place, *operands, scratch_shapes=(), cost=None, outputs=pltpu.VMEM):
    vmem = pl.BlockSpec(memory_space=pltpu.VMEM)
    return pl.pallas_call(
        kernel,
        out_shape=out_shape,
        in_specs=[pl.BlockSpec(memory_space=pltpu.SMEM)] + [vmem] * len(operands),
        out_specs=jax.tree.map(lambda _: pl.BlockSpec(memory_space=outputs), out_shape),
        scratch_shapes=scratch_shapes,
        cost_estimate=cost,
        compiler_params=pltpu.CompilerParams(vmem_limit_bytes=VMEM_BYTES),
    )(place, *operands)


def tri_at(z, wide):
    return wide * (z * (z + 1) // 2)


def pack_kernel(place_ref, *refs):
    pieces, out_ref = refs[:-1], refs[-1]
    chips, wide = len(pieces), pieces[0].shape[1] // len(pieces)
    height = out_ref.shape[0]
    for s in range(chips):
        for owner in range(chips):

            @pl.when(place_ref[0] ^ s == owner)
            def _(s=s, owner=owner):
                depth = wide * (owner + 1)
                for panel in range(2):
                    left = panel * tri_at(chips, wide) + tri_at(owner, wide)
                    rows = slice(panel * height, (panel + 1) * height)
                    out_ref[:, left : left + depth] = pieces[s][rows, :depth]


def pack_rows(place, pieces, cost):
    height, pb = pieces[0].shape[0] // 2, pieces[0].shape[1]
    width = 2 * tri_at(len(pieces), pb // len(pieces))
    out_shape = jax.ShapeDtypeStruct((height, width), jnp.bfloat16)
    return call(pack_kernel, out_shape, place, *pieces, cost=cost_of(cost))


def unpack_kernel(chips, rows_dev, place_ref, *refs):
    packs, out_ref = refs[:-1], refs[-1]
    cols = len(packs) // 2
    k, c = place_ref[1], place_ref[2]
    height, wide = packs[0].shape[0], out_ref.shape[2] // chips
    for at, pack in enumerate(packs):
        core = k if at < cols else 1 - k
        row = core * rows_dev + plane_owner(c, at % cols, cols, core) * height
        for z in range(chips):
            rows = pl.ds(pl.multiple_of(z * 2 * rows_dev + row, height), height)
            for panel in range(2):
                left, depth = panel * tri_at(chips, wide) + tri_at(z, wide), wide * (z + 1)
                out_ref[panel, rows, :depth] = pack[:, left : left + depth]


def unpack_rows(place, packs, chips, rows_dev, pb):
    out_shape = jax.ShapeDtypeStruct((2, pb, pb), jnp.bfloat16)
    return call(functools.partial(unpack_kernel, chips, rows_dev), out_shape, place, *packs)


def lower_product(place_ref, inverse, blocks, out_ref, right):
    z, k = place_ref[0], place_ref[1]
    rows_dev = blocks[0].shape[0] // 2
    for s, block in enumerate(blocks):
        for part, core in ((0, k), (1, 1 - k)):
            row = pl.multiple_of((z ^ s) * 2 * rows_dev + core * rows_dev, rows_dev)
            right[pl.ds(row, rows_dev), :] = block[part * rows_dev : (part + 1) * rows_dev, :]
    step = 2 * rows_dev
    for top in range(0, right.shape[0], step):
        out_ref[top : top + step, :] = product(
            inverse[top : top + step, : top + step], right[: top + step, :]
        ).astype(out_ref.dtype)


def first_kernel(place_ref, inverse, mine, theirs, below, *refs):
    blocks, (first, *carried, right) = refs[: -2 - CHUNKS], refs[-2 - CHUNKS :]
    lower_product(place_ref, inverse.at[0], blocks, first, right)
    width = carried[0].shape[1]
    rows_dev = mine.shape[0]
    for part, coupling in enumerate((mine, theirs)):
        rows = slice(part * rows_dev, (part + 1) * rows_dev)
        new = below[rows, :].astype(jnp.float32) - product(coupling[...], first[...])
        for chunk, out in enumerate(carried):
            out[rows, :] = new[:, chunk * width : (chunk + 1) * width].astype(out.dtype)


def second_kernel(place_ref, inverse, *refs):
    blocks, (second, right) = refs[:-2], refs[-2:]
    lower_product(place_ref, inverse.at[1], blocks, second, right)


def trailing_rows(panel, place_ref, total, factors, mine, theirs, out, done=None):
    k, c = place_ref[1], place_ref[2]
    cols = len(factors)
    depth, width = factors[0].shape[1], out.shape[1] // 2
    step, wide = min(256, out.shape[0]), mine[0].shape[1]
    for which in (0, 1):
        for upper in (0, 1):

            @pl.when(jnp.logical_and(k == which, c // (cols // 2) == upper))
            def _(which=which, upper=upper):
                at = plane_bits(cols, which).index(cols // 2)
                held = [m for m in range(cols) if m >> at & 1 == upper ^ panel]
                tops = [plane_owner(c, m, cols, which) % (cols // 2) * depth for m in held]
                tops = [pl.multiple_of(top, depth) for top in tops]
                for top in range(0, out.shape[0], step):
                    rows = slice(top, top + step)
                    left = jnp.concatenate([factors[m][rows, :] for m in held], axis=1)
                    for x, core in ((mine, which), (theirs, 1 - which)):
                        for chunk, part in enumerate(x):
                            right = [part[pl.ds(row, depth), :] for row in tops]
                            left_at = core * width + chunk * wide
                            columns = slice(left_at, left_at + wide)
                            out[rows, columns] = (
                                total[rows, columns].astype(jnp.float32)
                                - product(left, jnp.concatenate(right, axis=0))
                            ).astype(out.dtype)
                    if done:
                        done(rows)


def total_kernel(place_ref, rhs, *refs):
    factors, (mine, theirs, total) = refs[:-3], refs[-3:]
    trailing_rows(0, place_ref, rhs, factors, [mine], [theirs], total)


def last_kernel(place_ref, total, first, first_theirs, *refs):
    updated, solved, new_rows, new_solved, row_sems, solved_sem = refs[-6:]
    factors, x = refs[: -6 - 2 * CHUNKS], refs[-6 - 2 * CHUNKS : -6]
    second, second_theirs = x[:CHUNKS], x[CHUNKS:]
    z, k = place_ref[0], place_ref[1]
    rows_dev, width = solved.shape[1], first.shape[1]
    own = pl.ds(pl.multiple_of((2 * z + k) * rows_dev, rows_dev), rows_dev)
    panels = (([first], [first_theirs]), (second, second_theirs))
    for panel, halves in enumerate(panels):
        for half, core in zip(halves, (k, 1 - k)):
            wide = half[0].shape[1]
            for chunk, part in enumerate(half):
                left = pl.multiple_of(core * width + chunk * wide, wide)
                new_solved[panel, :, pl.ds(left, wide)] = part[own, :]
    store_solved = pltpu.make_async_copy(new_solved, solved, solved_sem)
    store_solved.start()
    step = updated.shape[0] // row_sems.shape[0]

    def store(rows):
        return pltpu.make_async_copy(
            new_rows.at[rows], updated.at[rows], row_sems.at[rows.start // step]
        )

    def done(rows):
        store(rows).start()

    trailing_rows(1, place_ref, total, factors, second, second_theirs, new_rows, done)
    for top in range(0, updated.shape[0], step):
        store(slice(top, top + step)).wait()
    store_solved.wait()


def by_permutes(sizes, rhs_top, diag_inverse, panel_coupling, trailing_factor, rhs_trailing):
    rows, cols = sizes
    chips = rows // 2
    rows_dev, pb = diag_inverse.shape[1:]
    half = rhs_top.shape[2] // 2
    wide = half // CHUNKS
    height = rows_dev // cols
    r, c = lax.axis_index("row"), lax.axis_index("col")
    z, k = r // 2, r % 2
    place = jnp.stack([z, k, c]).astype(jnp.int32)
    far, near = bits_of(chips)

    def along(x, s):
        return send(x, sizes, lambda r, c: (r ^ (2 * s), c))

    def across(x, i):
        return send(x, sizes, lambda r, c: (r, c ^ plane_bits(cols, r % 2)[i]))

    def swap(x):
        return send(x, sizes, lambda r, c: (r ^ 1, c))

    def block(*shape, dtype=jnp.bfloat16):
        return jax.ShapeDtypeStruct(shape, dtype)

    def share_of(matrices):
        mine = lax.dynamic_slice_in_dim(matrices, c * height, height, 1)
        return mine.reshape(2 * height, pb)

    def columns(core):
        return lax.dynamic_slice_in_dim(after(rhs_top, share), core * half, half, 2)

    def first_and_carried(*args):
        return call(
            first_kernel,
            [block(pb, half)] + [block(2 * rows_dev, wide)] * CHUNKS,
            place,
            *args,
            scratch_shapes=[pltpu.VMEM((pb, half), jnp.bfloat16)],
            cost=cost_of(0),
        )

    def second_of(*args):
        scratch = [pltpu.VMEM((pb, wide), jnp.bfloat16)]
        return call(second_kernel, block(pb, wide), place, *args, scratch_shapes=scratch)

    def total_of(*args):
        out_shape = block(*rhs_trailing.shape, dtype=jnp.float32)
        return call(total_kernel, out_shape, place, rhs_trailing, *args, cost=cost_of(4))

    def outputs_of(*args):
        out_shape = [block(*rhs_trailing.shape), block(2, rows_dev, 2 * half)]
        n_stores = max(rhs_trailing.shape[0] // 256, 1)
        scratch = [pltpu.VMEM(out.shape, out.dtype) for out in out_shape]
        scratch += [pltpu.SemaphoreType.DMA((n_stores,)), pltpu.SemaphoreType.DMA]
        return call(last_kernel, out_shape, place, *args, scratch_shapes=scratch, outputs=pl.ANY)

    share = share_of(diag_inverse)
    share_far = along(share, far)
    share_near = along(share, near)
    share_last = along(after(share_far, share_near), near)
    pack = pack_rows(place, [share, share_near, share_far, share_last], 2)
    pack_a = across(pack, 0)
    pack_b = across(pack, 1)
    pack_theirs = swap(pack)
    pack_a_theirs = swap(pack_a)
    pack_b_theirs = swap(pack_b)
    swapped = swap(columns(1 - k))
    chip_rhs = jnp.concatenate([columns(k), swapped], axis=1)
    top_far = along(after(chip_rhs, share_far)[0], far)
    top_near = along(after(chip_rhs, share_last)[0], near)
    top_last = along(top_far, near)
    coupling_theirs = swap(after(panel_coupling, top_far))
    pack_ab = across(after(pack_a, (coupling_theirs, pack_b, top_near)), 1)
    pack_ab_theirs = swap(pack_ab)
    inverse = unpack_rows(
        place,
        [
            pack,
            pack_a,
            pack_b,
            pack_ab,
            pack_theirs,
            pack_a_theirs,
            pack_b_theirs,
            after(pack_ab_theirs,
            top_last),
        ],
        chips,
        rows_dev,
        pb,
    )
    first_carried = first_and_carried(
        inverse,
        panel_coupling,
        coupling_theirs,
        chip_rhs[1],
        chip_rhs[0],
        top_near,
        top_far,
        top_last,
    )
    first = first_carried[0]
    first_theirs = swap(after(first, top_last))
    carried_0 = first_carried[1]
    carried_far_0 = along(carried_0, far)
    carried_near_0 = along(carried_0, near)
    factor_a = across(after(trailing_factor, share), 0)
    factor_b = across(after(trailing_factor, (coupling_theirs, factor_a)), 1)
    carried_last_0 = along(after(carried_far_0, (carried_near_0, factor_b, first_theirs)), near)
    second_0 = second_of(inverse, carried_0, carried_near_0, carried_far_0, carried_last_0)
    second_0_theirs = swap(second_0)
    factor_ab = across(after(factor_a, (factor_b, pack_ab)), 1)
    total = total_of(trailing_factor, factor_a, factor_b, factor_ab, first, first_theirs)
    outputs = outputs_of(
        total,
        first,
        first_theirs,
        trailing_factor,
        factor_a,
        factor_b,
        factor_ab,
        second_0,
        second_0_theirs,
    )
    updated, solved = outputs
    return solved, updated


def by_gathers(rhs_top, diag_inverse, panel_coupling, trailing_factor, rhs_trailing):
    def whole(x):
        return lax.all_gather(x, "row", axis=0, tiled=True)

    first = product(diag_inverse[0], whole(rhs_top[0])).astype(jnp.bfloat16)
    first_all = whole(first)
    carried = rhs_top[1].astype(jnp.float32) - product(panel_coupling, first_all)
    second = product(diag_inverse[1], whole(carried.astype(jnp.bfloat16))).astype(jnp.bfloat16)
    x = jnp.concatenate([first_all, whole(second)], axis=0)
    factor = lax.all_gather(trailing_factor, "col", axis=1, tiled=True)
    updated = (rhs_trailing.astype(jnp.float32) - product(factor, x)).astype(jnp.bfloat16)
    return jnp.stack([first, second]), updated


def fits(sizes, rhs_top, diag_inverse):
    rows, cols = sizes
    whole_rows = diag_inverse.shape[1] % (16 * cols) == 0
    whole_columns = diag_inverse.shape[2] % (64 * rows) == 0 and rhs_top.shape[2] % 256 == 0
    return rows == 8 and cols == 4 and whole_rows and whole_columns


def solution(mesh):
    sizes = (mesh.shape["row"], mesh.shape["col"])

    def shards(rhs_top, diag_inverse, *others):
        if fits(sizes, rhs_top, diag_inverse):
            return by_permutes(sizes, rhs_top, diag_inverse, *others)
        return by_gathers(rhs_top, diag_inverse, *others)

    in_specs = (
        P(None, "row", "col"),
        P(None, "row", None),
        P("row", None),
        P("row", "col"),
        P("row", "col"),
    )
    out_specs = (P(None, "row", "col"), P("row", "col"))
    return jax.shard_map(shards, mesh=mesh, in_specs=in_specs, out_specs=out_specs, check_vma=False)
```
